32 devices in a mesh: probe: 4 (over y, x), sht: 8 (over z, core).
Axes of the slice: x: 2, y: 2, z: 4, core: 2. Of those that a mesh axis runs over, the one named last changes fastest.
Arguments:
- legendre: bfloat16 [512, 512, 1025], P('sht', 'probe'), may hold values from -0.005859375 to 0.005859375
- pair_slots: int32 [512], replicated, may hold values from 0 to 511, each once
- cycle_slots: int32 [1024], replicated, may hold values from 0 to 1023, each once
- right_side: float32 [512, 2, 8, 1025], P('sht', None, 'probe'), may hold values from -24 to 24
- inv_spectrum: float32 [1024], replicated, may hold values from 0.3 to 3
- noise_level: float32 [1024], replicated, may hold values from 0.3 to 3
- inv_noise: float32 [1024, 2048], P('sht'), may hold values from 0.2 to 5
- pixel_mask: int32 [1024, 2048], P('sht'), may hold values 0 or 1
Outputs:
- solution: float32 [512, 2, 8, 1025], P('sht', None, 'probe')
- residual: float32 [512, 2, 8, 1025], P('sht', None, 'probe')
- direction: float32 [512, 2, 8, 1025], P('sht', None, 'probe')
The draws below stay inside these ranges and needn't reach their ends.
Inputs may be any that keep to these rules, and one draw needn't show every extreme that they name: Slot q holds the orders pair_slots[q] and 1023 - pair_slots[q]; every pair once. `cycle_slots`: each latitude cycle once. `pixel_mask`: 1 marks an observed pixel.
All inputs are finite; a program needn't handle non-finite values. No bound on the sum of `pixel_mask` on one device may be relied on, other than what follows from the above.
Results may differ from the reference program's by a relative error of at most 0.0043.
Values may be sent and summed in bfloat16 or wider, within the bound.
A program may use at most 192 MiB of HBM per device.

```python
import math
import jax
import jax.numpy as jnp
from jax import lax

L = 1024
NPHI = 2048
ROWS = 1025
PAIRS = 512
PROBES = 8
CYCLES = 1024
NORTH = 512


def draw_right_side(key, part):
    base_key = jax.random.fold_in(jax.random.fold_in(key, 11), 0)
    full_shape = (PAIRS, 2, PROBES, ROWS)
    slot_scale = jnp.exp(jnp.log(10.0) * jnp.arange(PAIRS, dtype=jnp.float32) / (PAIRS - 1)) / jnp.sqrt(10.0)
    values = jnp.clip(jax.random.normal(base_key, full_shape, jnp.float32), -6.0, 6.0)
    return values * slot_scale[:, None, None, None]


def plant(drawn, stream_key, least, largest):
    dims = drawn.shape
    spot = [jax.random.randint(jax.random.fold_in(stream_key, axis), (), 0, dims[axis]) for axis in range(len(dims))]
    drawn = drawn.at[tuple(spot)].set(least)
    longest = dims.index(max(dims))
    spot[longest] = (spot[longest] + 1) % dims[longest]
    return drawn.at[tuple(spot)].set(largest)


def block_scale(own_key, extent, cuts, smallest, top_value):
    def one(position, blocks):
        heights = jax.random.uniform(jax.random.fold_in(jax.random.fold_in(own_key, 6), position), (blocks,), jnp.float32, smallest / len(cuts), top_value / len(cuts))
        return jnp.repeat(jnp.exp(heights), extent[position] // blocks).reshape((-1,) + (1,) * (len(extent) - position - 1))

    loudness = one(*cuts[0])
    for cut in cuts[1:]:
        loudness = loudness * one(*cut)
    return loudness


def noise(rng, shape, width, most, cuts=(), kind=jnp.bfloat16):
    loudness = block_scale(rng, shape, cuts, -0.22, 0.18) if cuts else 1.0
    values = jax.random.normal(rng, shape, jnp.float32) * width * loudness
    return jnp.minimum(jnp.maximum(values, -most), most).astype(kind)


def setup_inputs(seed: int = 0) -> dict:
    arg_keys = jax.random.split(jax.random.key(seed), 9)
    return {
        "legendre": noise(arg_keys[0], (PAIRS, NORTH, ROWS), (CYCLES * L) ** -0.5, 0.005859375, ((0, 8), (1, 4))),
        "pair_slots": jax.random.permutation(arg_keys[1], PAIRS).astype(jnp.int32),
        "cycle_slots": jax.random.permutation(arg_keys[2], CYCLES).astype(jnp.int32),
        "right_side": draw_right_side(jax.random.fold_in(arg_keys[8], 71), 0),
        "inv_spectrum": jnp.clip(jnp.exp(jax.random.uniform(arg_keys[4], (L,), jnp.float32, math.log(0.3), math.log(3.0))), 0.3, 3.0),
        "noise_level": jnp.clip(jnp.exp(jax.random.uniform(arg_keys[5], (L,), jnp.float32, math.log(0.3), math.log(3.0))), 0.3, 3.0),
        "inv_noise": jnp.clip(jnp.exp(math.log(5.0) - 3.218876 * jax.random.uniform(arg_keys[6], (CYCLES, NPHI), jnp.float32) ** block_scale(arg_keys[6], (CYCLES, NPHI), ((0, 8),), -0.2, 0.2)), 0.2, 5.0),
        "pixel_mask": plant((jax.random.randint(arg_keys[7], (CYCLES, NPHI), 0, 5) < 4).astype(jnp.int32), jax.random.fold_in(arg_keys[7], 1), 0, 1),
    }


def row_factors(pair_slots):
    row_number = jnp.arange(ROWS, dtype=jnp.int32)[None, :]
    pair_value = pair_slots[:, None]
    first_seg = row_number < L - pair_value
    degree = jnp.where(first_seg, pair_value + row_number, row_number - 1)
    order_value = jnp.where(first_seg, pair_value, L - 1 - pair_value)
    parity = 1.0 - 2.0 * ((degree + order_value) % 2).astype(jnp.float32)
    first_mask = first_seg.astype(jnp.float32)
    second_mask = 1.0 - first_mask
    return jnp.stack([first_mask, first_mask * parity, second_mask, second_mask * parity], axis=1)

def packed_lookup(values, pair_slots):
    longer = jnp.concatenate([values, jnp.zeros((ROWS,), values.dtype)])
    first_part = jax.vmap(lambda offset: lax.dynamic_slice(longer, (offset,), (ROWS,)))(pair_slots.astype(jnp.int32))
    second = jnp.concatenate([jnp.zeros((1,), values.dtype), values])
    row_number = jnp.arange(ROWS, dtype=jnp.int32)[None, :]
    return jnp.where(row_number < (L - pair_slots)[:, None], first_part, second[None, :])

def blocked(array, block_size):
    return array.reshape((array.shape[0] // block_size, block_size) + array.shape[1:])

def legendre_forward(lowered, legendre, factors):
    block_size = math.gcd(PAIRS, 32)

    def one_block(pieces):
        source, tile_rows, sign_rows = pieces
        spread = source.astype(jnp.float32)[:, None] * sign_rows[:, :, None, None, :]
        return jnp.einsum('qvcpr,qjr->qjvcp', spread, tile_rows.astype(jnp.float32))
    result = lax.map(one_block, (blocked(lowered, block_size), blocked(legendre, block_size), blocked(factors, block_size)))
    return result.reshape((PAIRS, NORTH, 4, 2, PROBES))

def legendre_adjoint(cotangent, legendre, factors):
    block_size = math.gcd(PAIRS, 32)

    def one_block(pieces):
        source, tile_rows, sign_rows = pieces
        pulled = jnp.einsum('qjvcp,qjr->qvcpr', source.astype(jnp.float32), tile_rows.astype(jnp.float32))
        return lax.optimization_barrier(jnp.sum(pulled * sign_rows[:, :, None, None, :], axis=1))
    result = lax.map(one_block, (blocked(cotangent, block_size), blocked(legendre, block_size), blocked(factors, block_size)))
    return result.reshape((PAIRS, 2, PROBES, ROWS))

def reference(legendre, pair_slots, cycle_slots, right_side, inv_spectrum, noise_level, inv_noise, pixel_mask):
    factors = row_factors(pair_slots)
    inverse_signal = packed_lookup(inv_spectrum, pair_slots)[:, None, None, :]
    precond = 1.0 / (inverse_signal + packed_lookup(noise_level, pair_slots)[:, None, None, :])
    precond_rhs = precond * right_side
    start_norm = lax.optimization_barrier(jnp.sum(right_side * precond_rhs, axis=(0, 1, 3)))
    lowered = precond_rhs.astype(jnp.bfloat16)
    coeffs = legendre_forward(lowered, legendre, factors)
    seg_first = jnp.concatenate([coeffs[:, :, 0], coeffs[:, ::-1, 1]], axis=1)
    seg_second = jnp.concatenate([coeffs[:, :, 2], coeffs[:, ::-1, 3]], axis=1)

    def to_pixels(first_seg, second_seg):
        spectra = jnp.zeros((L, CYCLES, 2, PROBES), first_seg.dtype)
        spectra = spectra.at[pair_slots].set(first_seg).at[L - 1 - pair_slots].set(second_seg)
        complex_modes = spectra[:, :, 0] + 1j * spectra[:, :, 1]
        padded = jnp.concatenate([complex_modes, jnp.zeros((NPHI - L, CYCLES, PROBES), complex_modes.dtype)], axis=0)
        pixels = jnp.real(jnp.fft.ifft(padded, axis=0)) * NPHI
        return jnp.take(pixels, cycle_slots, axis=1)
    pixels, pullback = jax.vjp(to_pixels, seg_first, seg_second)
    weight = (inv_noise * pixel_mask.astype(jnp.float32)).T
    back_first, back_second = pullback(pixels * weight[:, :, None])
    cotangent = jnp.stack([back_first[:, :NORTH], back_first[:, NORTH:][:, ::-1], back_second[:, :NORTH], back_second[:, NORTH:][:, ::-1]], axis=2).astype(jnp.bfloat16)
    noise_term = legendre_adjoint(cotangent, legendre, factors)
    operator_image = inverse_signal * precond_rhs + noise_term
    curvature = lax.optimization_barrier(jnp.sum(precond_rhs * operator_image, axis=(0, 1, 3)))
    step_size = (start_norm / curvature)[None, None, :, None]
    solution = step_size * precond_rhs
    residual = right_side - step_size * operator_image
    precond_res = precond * residual
    new_norm = lax.optimization_barrier(jnp.sum(residual * precond_res, axis=(0, 1, 3)))
    direction = precond_res + (new_norm / start_norm)[None, None, :, None] * precond_rhs
    return (solution, residual, direction)
```

```python
import math

import jax
import jax.numpy as jnp
import ml_dtypes
import numpy as np
from jax import lax
from jax.experimental import pallas as pl
from jax.experimental.pallas import tpu as pltpu
from jax.sharding import PartitionSpec as P

L = 1024
NPHI = 2048
ROWS = 1025
PAIRS = 512
HALF = NPHI // 2
WIDE = 2048
BF = jnp.bfloat16
F32 = jnp.float32


def fourier_tables():
    k = np.arange(HALF)[:, None]
    tables = []
    for parity in range(2):
        m = np.arange(parity, L, 2)[None, :]
        angle = (k * m % NPHI) * (2.0 * math.pi / NPHI)
        tables.append(np.concatenate([np.cos(angle), -np.sin(angle)], axis=1))
    exact = np.stack(tables)
    high = exact.astype(ml_dtypes.bfloat16)
    low = (exact - high.astype(np.float64)).astype(ml_dtypes.bfloat16)
    return high, low


def lookup_kernel(count, orders_ref, first_ref, second_ref, inverse_ref, precond_ref):
    lane = lax.broadcasted_iota(jnp.int32, (8, WIDE), 1)
    first = first_ref[...]
    second = second_ref[...]
    for slot in range(count):
        pair = orders_ref[slot]
        turned = pltpu.roll(first, lax.rem(WIDE - pair, WIDE), 1)
        row = jnp.where(lane < L - pair, turned, second)
        inverse_ref[slot : slot + 1, :] = row[0:1, :ROWS]
        precond_ref[slot : slot + 1, :] = (1.0 / (row[0:1] + row[1:2]))[:, :ROWS]


def packed_tables(inv_spectrum, noise_level, local_orders):
    count = local_orders.shape[0]
    both = jnp.stack([inv_spectrum, noise_level])
    first = jnp.pad(both, ((0, 6), (0, WIDE - L)), constant_values=1.0)
    second = jnp.pad(both, ((0, 6), (1, WIDE - L - 1)), constant_values=1.0)
    return pl.pallas_call(
        lambda *refs: lookup_kernel(count, *refs),
        out_shape=[jax.ShapeDtypeStruct((count, ROWS), F32)] * 2,
        in_specs=[
            pl.BlockSpec(memory_space=pltpu.SMEM),
            pl.BlockSpec(memory_space=pltpu.VMEM),
            pl.BlockSpec(memory_space=pltpu.VMEM),
        ],
        out_specs=[pl.BlockSpec(memory_space=pltpu.VMEM)] * 2,
        name="packed_lookup",
    )(local_orders, first, second)


def dot(equation, left, right):
    return jnp.einsum(equation, left, right, preferred_element_type=F32)


def shards(
    legendre, pair_slots, cycle_slots, right_side, inv_spectrum, noise_level, inv_noise, pixel_mask
):
    local_pairs, local_north = legendre.shape[:2]
    probe_size = lax.axis_size("probe")
    sht_size = lax.axis_size("sht")
    local_probes = right_side.shape[2]
    probes = local_probes * probe_size
    north = local_north * probe_size
    probe_cuts = math.gcd(probes, sht_size)
    cycle_cuts = sht_size // probe_cuts
    inner_probes = probes // probe_cuts
    inner_north = local_north // cycle_cuts
    columns = 2 * inner_probes * inner_north
    sht = lax.axis_index("sht")
    probe = lax.axis_index("probe")

    weight = jnp.where(pixel_mask != 0, inv_noise, 0.0).astype(BF)
    all_weights = lax.all_gather(weight, "sht", axis=0, tiled=True)

    local_orders = lax.dynamic_slice_in_dim(pair_slots, sht * local_pairs, local_pairs)
    inverse_rows, precond_rows = packed_tables(inv_spectrum, noise_level, local_orders)
    inverse_signal = inverse_rows[:, None, None, :]
    precond = precond_rows[:, None, None, :]
    precond_rhs = precond * right_side
    lowered = precond_rhs.astype(BF)
    gathered = lax.all_gather(lowered, "probe", axis=2, tiled=True)

    row = jnp.arange(ROWS, dtype=jnp.int32)[None, :]
    pair = local_orders[:, None]
    first_mask = (row < L - pair).astype(F32)
    second_mask = 1.0 - first_mask
    first_sign = (1 - 2 * (row % 2)).astype(F32)
    second_sign = (1 - 2 * ((row + pair) % 2)).astype(F32)
    factors = jnp.stack(
        [first_mask, first_mask * first_sign, second_mask, second_mask * second_sign], axis=1
    )
    spread = gathered[:, None] * factors[:, :, None, None, :].astype(BF)
    coeffs = dot("qvcpr,qjr->qvcpj", spread, legendre).astype(BF)

    outgoing = coeffs.reshape(
        local_pairs, 2, 2, 2, probe_cuts, inner_probes, cycle_cuts, inner_north
    ).transpose(4, 6, 3, 0, 1, 2, 5, 7)
    outgoing = outgoing.reshape(sht_size, 2, 2 * local_pairs, columns)
    received = lax.all_to_all(outgoing, "sht", split_axis=0, concat_axis=0, tiled=True)

    order = jnp.arange(L, dtype=jnp.int32)
    order = (order % (L // 2)) * 2 + order // (L // 2)
    slot_orders = jnp.stack([pair_slots, L - 1 - pair_slots], axis=1).reshape(
        sht_size, 2 * local_pairs
    )
    place = (order[:, None, None] == slot_orders[None]).astype(BF)
    spectra = dot("msq,scqn->cmn", place, received).astype(BF)
    spectra = spectra.reshape(2, 2, L // 2, columns).transpose(1, 0, 2, 3).reshape(2, L, columns)

    north_here = (
        probe * local_north
        + (sht % cycle_cuts) * inner_north
        + jnp.arange(inner_north, dtype=jnp.int32)
    )
    cycles = jnp.stack([north_here, 2 * north - 1 - north_here])
    cycles = jnp.broadcast_to(cycles[:, None, :], (2, inner_probes, inner_north)).reshape(columns)
    pick = (cycle_slots[:, None] == cycles[None, :]).astype(BF)
    here_weight = dot("sk,sn->kn", all_weights, pick)

    high, low = fourier_tables()
    high, low = jnp.asarray(high), jnp.asarray(low)
    parts = dot("akx,axn->akn", high, spectra) + dot("akx,axn->akn", low, spectra)
    near = here_weight[:HALF] * (parts[0] + parts[1])
    far = here_weight[HALF:] * (parts[0] - parts[1])
    weighted = jnp.stack([near + far, near - far]).astype(BF)
    back = dot("akx,akn->axn", high, weighted) + dot("akx,akn->axn", low, weighted)
    back = back.astype(BF).reshape(2, 2, L // 2, columns).transpose(1, 0, 2, 3).reshape(2, L, columns)
    returning = dot("msq,cmn->scqn", place, back).astype(BF)
    returned = lax.all_to_all(returning, "sht", split_axis=0, concat_axis=0, tiled=True)
    cotangent = (
        returned.reshape(
            probe_cuts, cycle_cuts, 2, local_pairs, 2, 2, inner_probes, inner_north
        )
        .transpose(3, 4, 5, 2, 0, 6, 1, 7)
        .reshape(local_pairs, 4, 2, probes, local_north)
    )
    pulled = dot("qvcpj,qjr->qvcpr", cotangent, legendre)
    partial = jnp.sum(pulled * factors[:, :, None, None, :], axis=1)
    partial = partial.astype(BF).reshape(local_pairs, 2, probe_size, local_probes, ROWS)
    pieces = lax.all_to_all(
        partial.transpose(2, 0, 1, 3, 4), "probe", split_axis=0, concat_axis=0, tiled=True
    )
    noise_term = jnp.sum(pieces.astype(F32), axis=0)

    operator_image = inverse_signal * precond_rhs + noise_term
    start_local = jnp.sum(right_side * precond_rhs, axis=(0, 1, 3))
    curve_local = jnp.sum(precond_rhs * operator_image, axis=(0, 1, 3))
    image_local = jnp.sum(operator_image * precond * operator_image, axis=(0, 1, 3))
    start_norm, curvature, image_norm = lax.psum((start_local, curve_local, image_local), "sht")
    step_size = start_norm / curvature
    residual = right_side - step_size[None, None, :, None] * operator_image
    new_norm = start_norm - 2.0 * step_size * curvature + step_size * step_size * image_norm
    answer = step_size[None, None, :, None] * precond_rhs
    direction = precond * residual + (new_norm / start_norm)[None, None, :, None] * precond_rhs
    return (answer, residual, direction)


def solution(mesh):
    placed = (
        P("sht", "probe", None),
        P(),
        P(),
        P("sht", None, "probe", None),
        P(),
        P(),
        P("sht", None),
        P("sht", None),
    )
    return jax.shard_map(
        shards,
        mesh=mesh,
        in_specs=placed,
        out_specs=(P("sht", None, "probe", None),) * 3,
        check_vma=False,
    )
```

```python
import math

import jax
import jax.numpy as jnp
import ml_dtypes
import numpy as np
from jax import lax
from jax.experimental import pallas as pl
from jax.experimental.pallas import tpu as pltpu
from jax.sharding import PartitionSpec as P

L = 1024
NPHI = 2048
ROWS = 1025
PAIRS = 512
HALF = NPHI // 2
WIDE = 2048
BF = jnp.bfloat16
F32 = jnp.float32


def fourier_tables():
    k = np.arange(HALF)[:, None]
    tables = []
    for parity in range(2):
        m = np.arange(parity, L, 2)[None, :]
        angle = (k * m % NPHI) * (2.0 * math.pi / NPHI)
        tables.append(np.concatenate([np.cos(angle), -np.sin(angle)], axis=1))
    exact = np.stack(tables)
    high = exact.astype(ml_dtypes.bfloat16)
    low = (exact - high.astype(np.float64)).astype(ml_dtypes.bfloat16)
    return high, low


def lookup_kernel(count, orders_ref, first_ref, second_ref, inverse_ref, precond_ref):
    lane = lax.broadcasted_iota(jnp.int32, (8, WIDE), 1)
    first = first_ref[...]
    second = second_ref[...]
    for slot in range(count):
        pair = orders_ref[slot]
        turned = pltpu.roll(first, lax.rem(WIDE - pair, WIDE), 1)
        row = jnp.where(lane < L - pair, turned, second)
        inverse_ref[slot : slot + 1, :] = row[0:1, :ROWS]
        precond_ref[slot : slot + 1, :] = (1.0 / (row[0:1] + row[1:2]))[:, :ROWS]


def packed_tables(inv_spectrum, noise_level, local_orders):
    count = local_orders.shape[0]
    both = jnp.stack([inv_spectrum, noise_level])
    first = jnp.pad(both, ((0, 6), (0, WIDE - L)), constant_values=1.0)
    second = jnp.pad(both, ((0, 6), (1, WIDE - L - 1)), constant_values=1.0)
    return pl.pallas_call(
        lambda *refs: lookup_kernel(count, *refs),
        out_shape=[jax.ShapeDtypeStruct((count, ROWS), F32)] * 2,
        in_specs=[
            pl.BlockSpec(memory_space=pltpu.SMEM),
            pl.BlockSpec(memory_space=pltpu.VMEM),
            pl.BlockSpec(memory_space=pltpu.VMEM),
        ],
        out_specs=[pl.BlockSpec(memory_space=pltpu.VMEM)] * 2,
        name="packed_lookup",
    )(local_orders, first, second)


def exchange_kernel(axis, count, share, source, landed, send_sems, land_sems, own_sem):
    here = lax.axis_index(axis)
    peers = [lax.rem(here + step, count) for step in range(count)]
    barrier = pltpu.get_barrier_semaphore()
    for peer in peers[1:]:
        pl.semaphore_signal(
            barrier, inc=1, device_id={axis: peer}, device_id_type=pl.DeviceIdType.MESH
        )
    pl.semaphore_wait(barrier, count - 1)
    copies = []
    for step in range(1, count):
        copy = pltpu.make_async_remote_copy(
            src_ref=source if share else source.at[peers[step]],
            dst_ref=landed.at[here],
            send_sem=send_sems.at[step],
            recv_sem=land_sems.at[step],
            device_id={axis: peers[step]},
            device_id_type=pl.DeviceIdType.MESH,
        )
        copy.start()
        copies.append(copy)
    own = pltpu.make_async_copy(source if share else source.at[here], landed.at[here], own_sem)
    own.start()
    own.wait()
    for copy in copies:
        copy.wait()


def exchange(array, axis, number, share=False):
    count = lax.axis_size(axis)
    shape = (count,) + array.shape if share else array.shape
    return pl.pallas_call(
        lambda *refs: exchange_kernel(axis, count, share, *refs),
        out_shape=jax.ShapeDtypeStruct(shape, array.dtype),
        in_specs=[pl.BlockSpec(memory_space=pl.ANY)],
        out_specs=pl.BlockSpec(memory_space=pl.ANY),
        scratch_shapes=[
            pltpu.SemaphoreType.DMA((count,)),
            pltpu.SemaphoreType.DMA((count,)),
            pltpu.SemaphoreType.DMA,
        ],
        compiler_params=pltpu.CompilerParams(collective_id=number, has_side_effects=True),
        name="exchange_" + str(number),
    )(array)


def dot(equation, left, right):
    return jnp.einsum(equation, left, right, preferred_element_type=F32)


def shards(
    legendre, pair_slots, cycle_slots, right_side, inv_spectrum, noise_level, inv_noise, pixel_mask
):
    local_pairs, local_north = legendre.shape[:2]
    probe_size = lax.axis_size("probe")
    sht_size = lax.axis_size("sht")
    local_probes = right_side.shape[2]
    probes = local_probes * probe_size
    north = local_north * probe_size
    probe_cuts = math.gcd(probes, sht_size)
    cycle_cuts = sht_size // probe_cuts
    inner_probes = probes // probe_cuts
    inner_north = local_north // cycle_cuts
    columns = 2 * inner_probes * inner_north
    sht = lax.axis_index("sht")
    probe = lax.axis_index("probe")

    weight = jnp.where(pixel_mask != 0, inv_noise, 0.0).astype(BF)
    all_weights = lax.all_gather(weight, "sht", axis=0, tiled=True)

    local_orders = lax.dynamic_slice_in_dim(pair_slots, sht * local_pairs, local_pairs)
    inverse_rows, precond_rows = packed_tables(inv_spectrum, noise_level, local_orders)
    inverse_signal = inverse_rows[:, None, None, :]
    precond = precond_rows[:, None, None, :]
    precond_rhs = precond * right_side
    lowered = precond_rhs.astype(BF)
    gathered = exchange(lowered.reshape(-1, ROWS), "probe", 0, share=True)
    gathered = (
        gathered.reshape(probe_size, local_pairs, 2, local_probes, ROWS)
        .transpose(1, 2, 0, 3, 4)
        .reshape(local_pairs, 2, probes, ROWS)
    )

    row = jnp.arange(ROWS, dtype=jnp.int32)[None, :]
    pair = local_orders[:, None]
    first_mask = (row < L - pair).astype(F32)
    second_mask = 1.0 - first_mask
    first_sign = (1 - 2 * (row % 2)).astype(F32)
    second_sign = (1 - 2 * ((row + pair) % 2)).astype(F32)
    factors = jnp.stack(
        [first_mask, first_mask * first_sign, second_mask, second_mask * second_sign], axis=1
    )
    spread = gathered[:, None] * factors[:, :, None, None, :].astype(BF)
    coeffs = dot("qvcpr,qjr->qvcpj", spread, legendre).astype(BF)

    outgoing = coeffs.reshape(
        local_pairs, 2, 2, 2, probe_cuts, inner_probes, cycle_cuts, inner_north
    ).transpose(4, 6, 3, 0, 1, 2, 5, 7)
    received = exchange(outgoing.reshape(sht_size, 4 * local_pairs, columns), "sht", 1)
    received = received.reshape(sht_size, 2, 2 * local_pairs, columns)

    order = jnp.arange(L, dtype=jnp.int32)
    order = (order % (L // 2)) * 2 + order // (L // 2)
    slot_orders = jnp.stack([pair_slots, L - 1 - pair_slots], axis=1).reshape(
        sht_size, 2 * local_pairs
    )
    place = (order[:, None, None] == slot_orders[None]).astype(BF)
    spectra = dot("msq,scqn->cmn", place, received).astype(BF)
    spectra = spectra.reshape(2, 2, L // 2, columns).transpose(1, 0, 2, 3).reshape(2, L, columns)

    north_here = (
        probe * local_north
        + (sht % cycle_cuts) * inner_north
        + jnp.arange(inner_north, dtype=jnp.int32)
    )
    cycles = jnp.stack([north_here, 2 * north - 1 - north_here])
    cycles = jnp.broadcast_to(cycles[:, None, :], (2, inner_probes, inner_north)).reshape(columns)
    pick = (cycle_slots[:, None] == cycles[None, :]).astype(BF)
    here_weight = dot("sk,sn->kn", all_weights, pick)

    high, low = fourier_tables()
    high, low = jnp.asarray(high), jnp.asarray(low)
    parts = dot("akx,axn->akn", high, spectra) + dot("akx,axn->akn", low, spectra)
    near = here_weight[:HALF] * (parts[0] + parts[1])
    far = here_weight[HALF:] * (parts[0] - parts[1])
    weighted = jnp.stack([near + far, near - far]).astype(BF)
    back = dot("akx,akn->axn", high, weighted) + dot("akx,akn->axn", low, weighted)
    back = back.astype(BF).reshape(2, 2, L // 2, columns).transpose(1, 0, 2, 3).reshape(2, L, columns)
    returning = dot("msq,cmn->scqn", place, back).astype(BF)
    returned = exchange(returning.reshape(sht_size, 4 * local_pairs, columns), "sht", 2)
    cotangent = (
        returned.reshape(
            probe_cuts, cycle_cuts, 2, local_pairs, 2, 2, inner_probes, inner_north
        )
        .transpose(3, 4, 5, 2, 0, 6, 1, 7)
        .reshape(local_pairs, 4, 2, probes, local_north)
    )
    pulled = dot("qvcpj,qjr->qvcpr", cotangent, legendre)
    partial = jnp.sum(pulled * factors[:, :, None, None, :], axis=1)
    partial = partial.astype(BF).reshape(local_pairs, 2, probe_size, local_probes, ROWS)
    pieces = exchange(
        partial.transpose(2, 0, 1, 3, 4).reshape(probe_size, -1, ROWS), "probe", 3
    )
    noise_term = jnp.sum(pieces.astype(F32), axis=0).reshape(right_side.shape)

    operator_image = inverse_signal * precond_rhs + noise_term
    start_local = jnp.sum(right_side * precond_rhs, axis=(0, 1, 3))
    curve_local = jnp.sum(precond_rhs * operator_image, axis=(0, 1, 3))
    image_local = jnp.sum(operator_image * precond * operator_image, axis=(0, 1, 3))
    local_sums = jnp.stack([start_local, curve_local, image_local])
    padded_sums = jnp.pad(local_sums, ((0, 5), (0, 128 - local_probes)))
    all_sums = jnp.sum(exchange(padded_sums, "sht", 4, share=True), axis=0)
    start_norm, curvature, image_norm = (all_sums[i, :local_probes] for i in range(3))
    step_size = start_norm / curvature
    residual = right_side - step_size[None, None, :, None] * operator_image
    new_norm = start_norm - 2.0 * step_size * curvature + step_size * step_size * image_norm
    answer = step_size[None, None, :, None] * precond_rhs
    direction = precond * residual + (new_norm / start_norm)[None, None, :, None] * precond_rhs
    return (answer, residual, direction)


def solution(mesh):
    placed = (
        P("sht", "probe", None),
        P(),
        P(),
        P("sht", None, "probe", None),
        P(),
        P(),
        P("sht", None),
        P("sht", None),
    )
    return jax.shard_map(
        shards,
        mesh=mesh,
        in_specs=placed,
        out_specs=(P("sht", None, "probe", None),) * 3,
        check_vma=False,
    )
```
